256 devices in a mesh: ctx: 32 (over y_lo, z, core), head: 8 (over y_hi, x).
Axes of the slice: x: 4, y: 4 (y_hi: 2, y_lo: 2; y = y_hi * 2 + y_lo), z: 8, core: 2. Of those that a mesh axis runs over, the one named last changes fastest.
Arguments:
- queries: bfloat16 [32768, 1024], P(('ctx', 'head')), may hold values from -15 to 15
- keys: bfloat16 [32768, 128], P(('ctx', 'head')), may hold values from -12 to 12
- values: bfloat16 [32768, 128], P(('ctx', 'head')), may hold values from -6 to 6
- doc_lengths: int32 [16], replicated, may hold values from 1 to 17408, 32768 in all
Outputs:
- attended: bfloat16 [32768, 1024], P(('ctx', 'head'))
The draws below stay inside these ranges and needn't reach their ends.
Inputs may be any that keep to these rules, and one draw needn't show every extreme that they name: `doc_lengths`: the 16 lengths sum to 32768 and the largest is 17408.
All inputs are finite; a program needn't handle non-finite values.
Results may differ from the reference program's by a relative error of at most 0.0049.
Values may be sent and summed in bfloat16 or wider, within the bound.
A program may use at most 64 MiB of HBM per device.

```python
import math
import jax
import jax.numpy as jnp
import numpy as np
from jax import lax

HD = 128
QHEADS = 8
TOK_DEV = 128
NDOCS = 16
TOKENS = 32768
DOC_MOST = 17408
N_HEAD = 8


def steps_of(rng, shape, cuts, least, largest):
    level, own = 1.0, jax.random.fold_in(rng, 6)
    for axis_at, blocks in cuts:
        heights = jnp.exp(jax.random.uniform(jax.random.fold_in(own, axis_at), (blocks,), jnp.float32, least / len(cuts), largest / len(cuts)))
        level = level * jnp.repeat(heights, shape[axis_at] // blocks).reshape([-1 if axis == axis_at else 1 for axis in range(len(shape))])
    return level


def profile(amount, total, limit, lean):
    portions = [(1 << 20) // math.isqrt(rank ** lean) + 1 for rank in range(2, amount + 1)]
    surplus, holding = total - limit - (amount - 1), [1] * (amount - 1)
    while surplus > 0:
        candidates = [i for i in range(amount - 1) if holding[i] < limit]
        mass, remaining = sum([portions[i] for i in candidates]), surplus
        for i in candidates:
            addition = min(limit - holding[i], max(1, remaining * portions[i] // mass), surplus)
            holding[i] = holding[i] + addition
            surplus = surplus - addition
    return np.array([limit] + holding)


def uneven(stream_key, count, total, bound, slope):
    if count == 2:
        one = jax.random.randint(stream_key, (), max(1, total - bound), min(bound, total - 1) + 1)
        return jnp.stack([one, total - one])
    sizes = jnp.asarray(profile(count, total, bound, slope), jnp.int32)
    twos = (count - 1) // 2
    source_of, sink = sizes[1:1 + 2 * twos:2], sizes[2:2 + 2 * twos:2]
    margin = jnp.minimum(source_of - 1, bound - sink)
    shifted = jax.random.randint(jax.random.fold_in(stream_key, 1), (twos,), 0, 1 << 20) % (margin + 1)
    sizes = sizes.at[1:1 + 2 * twos:2].set(source_of - shifted).at[2:2 + 2 * twos:2].set(sink + shifted)
    return sizes[jax.random.permutation(jax.random.fold_in(stream_key, 2), count)]


def normal_values(stream_key, extent, scale, bound, shards=(), held_as=jnp.bfloat16):
    array = jax.random.normal(stream_key, extent, jnp.float32) * scale
    if len(shards) > 0:
        array = steps_of(stream_key, extent, shards, -0.22, 0.18) * array
    return jnp.clip(array, min=-bound, max=bound).astype(held_as)


def setup_inputs(seed: int = 0) -> dict:
    splits = jax.random.split(jax.random.key(seed), 5)
    return {
        "queries": normal_values(splits[0], (TOKENS, QHEADS * HD), 2.5, 15.0, ((0, 256),)),
        "keys": normal_values(splits[1], (TOKENS, HD), 2.0, 12.0, ((0, 256),)),
        "values": normal_values(splits[2], (TOKENS, HD), 1.0, 6.0, ((0, 256),)),
        "doc_lengths": uneven(splits[3], NDOCS, TOKENS, DOC_MOST, 2).astype(jnp.int32),
    }


def doc_starts(lengths, positions):
    ends = jnp.cumsum(lengths).astype(jnp.int32)
    chosen = jnp.where(ends[None, :] <= positions[:, None], lengths[None, :], 0)
    return lax.optimization_barrier(jnp.sum(chosen, axis=1)).astype(jnp.int32)

def reference(queries, keys, values, doc_lengths):
    positions = jnp.arange(TOKENS, dtype=jnp.int32)
    starts = doc_starts(doc_lengths, positions)
    block_rows = TOK_DEV * N_HEAD
    window = min(DOC_MOST + block_rows, TOKENS)
    block_total = TOKENS // block_rows
    factor = 1.0 / (30.0 * math.sqrt(HD))

    def attend_block(item):
        block_index = item // QHEADS
        head_index = item % QHEADS
        first_row = (block_index * block_rows).astype(jnp.int32)
        query_block = lax.dynamic_slice(queries, (first_row, (head_index * HD).astype(jnp.int32)), (block_rows, HD))
        key_first = jnp.clip(first_row - DOC_MOST, 0, TOKENS - window).astype(jnp.int32)
        key_block = lax.dynamic_slice(keys, (key_first, jnp.int32(0)), (window, HD))
        value_block = lax.dynamic_slice(values, (key_first, jnp.int32(0)), (window, HD))
        scores = jnp.dot(query_block, key_block.T, preferred_element_type=jnp.float32)
        capped = 30.0 * jnp.tanh(scores * factor)
        query_pos = first_row + jnp.arange(block_rows, dtype=jnp.int32)
        key_pos = key_first + jnp.arange(window, dtype=jnp.int32)
        row_start = lax.dynamic_slice(starts, (first_row,), (block_rows,))
        allowed = (key_pos[None, :] <= query_pos[:, None]) & (key_pos[None, :] >= row_start[:, None])
        weights = jnp.where(allowed, jnp.exp(capped), jnp.float32(0.0))
        numerator = jnp.dot(weights.astype(jnp.bfloat16), value_block, preferred_element_type=jnp.float32)
        denominator = lax.optimization_barrier(jnp.sum(weights, axis=1))
        return (numerator / denominator[:, None]).astype(jnp.bfloat16)
    blocks = lax.map(attend_block, jnp.arange(block_total * QHEADS, dtype=jnp.int32))
    blocks = blocks.reshape(block_total, QHEADS, block_rows, HD).transpose(0, 2, 1, 3)
    return blocks.reshape(TOKENS, QHEADS * HD)
```

```python
import functools
import math

import jax
import jax.numpy as jnp
from jax import lax
from jax.experimental import pallas as pl
from jax.experimental.pallas import tpu as pltpu
from jax.sharding import PartitionSpec as P

MESH = pl.DeviceIdType.MESH
HD = 128
HEADS = 8
TOK = 128
NDOCS = 16
ROWS = HEADS * TOK
FACTOR = 1.0 / (30.0 * math.sqrt(HD))
GAIN = 30.0 * math.log2(math.e)
PAD = 4
LAST = 34
SLOTS = PAD + LAST + 2


def rows_of(slot, count=1):
    first = (slot + PAD) * TOK
    if not isinstance(first, int):
        first = pl.multiple_of(first, TOK)
    return pl.ds(first, count * TOK)


def kernel(
    q_ref, k_ref, v_ref, len_ref, o_ref,
    kv, qbuf, starts, acc, osend, orecv, dsend, drecv,
    kv_recv, kv_send, q_recv, q_send, o_recv, o_send, d_recv, d_send,
):
    ctx = lax.axis_index("ctx")
    head = lax.axis_index("head")
    L = ctx // 2
    c = ctx % 2
    h = head // 4
    x = head % 4
    w = 2 * c + h
    u = 4 * L + w

    chain_next = (ctx + 2, head)
    chain_prev = (ctx - 2, head)
    yh_peer = (ctx, (1 - h) * 4 + x)
    sib_peer = (L * 2 + 1 - c, head)

    def x_peer(j):
        return (ctx, h * 4 + (x + j) % 4)

    kv[...] = jnp.zeros_like(kv)
    kv[rows_of(LAST), 0:HD] = k_ref[...]
    kv[rows_of(LAST), HD:] = v_ref[...]
    for a in range(HEADS):
        qbuf[0, a * TOK:(a + 1) * TOK, :] = q_ref[:, a * HD:(a + 1) * HD]

    barrier = pltpu.get_barrier_semaphore()
    for peer in (yh_peer, sib_peer, x_peer(1), x_peer(2), x_peer(3)):
        pl.semaphore_signal(barrier, inc=1, device_id=peer, device_id_type=MESH)

    @pl.when(L < 15)
    def _():
        pl.semaphore_signal(barrier, inc=1, device_id=chain_next, device_id_type=MESH)

    @pl.when(L > 0)
    def _():
        pl.semaphore_signal(barrier, inc=1, device_id=chain_prev, device_id_type=MESH)

    for j in range(4):
        pos = (4 * u + (x + j) % 4) * TOK + lax.broadcasted_iota(jnp.int32, (TOK, TOK), 0)
        end = jnp.int32(0)
        start = jnp.zeros((TOK, TOK), jnp.int32)
        for d in range(NDOCS):
            length = len_ref[d]
            end = end + length
            start = start + jnp.where(pos >= end, length, 0)
        starts[j] = start

    pl.semaphore_wait(barrier, 5 + (L < 15).astype(jnp.int32) + (L > 0).astype(jnp.int32))

    def q_copy(j):
        return pltpu.make_async_remote_copy(
            src_ref=qbuf.at[0], dst_ref=qbuf.at[j], send_sem=q_send.at[j - 1],
            recv_sem=q_recv.at[j - 1], device_id=x_peer(4 - j), device_id_type=MESH)

    def o_copy(j):
        return pltpu.make_async_remote_copy(
            src_ref=osend.at[j - 1], dst_ref=orecv.at[j - 1], send_sem=o_send.at[j - 1],
            recv_sem=o_recv.at[j - 1], device_id=x_peer(j), device_id_type=MESH)

    def d_copy(j):
        return pltpu.make_async_remote_copy(
            src_ref=dsend.at[j - 1], dst_ref=drecv.at[j - 1], send_sem=d_send.at[j - 1],
            recv_sem=d_recv.at[j - 1], device_id=x_peer(j), device_id_type=MESH)

    def kv_copy(src, dst, kind, k, peer):
        return pltpu.make_async_remote_copy(
            src_ref=kv.at[rows_of(src)], dst_ref=kv.at[rows_of(dst)], send_sem=kv_send.at[kind, k],
            recv_sem=kv_recv.at[dst + PAD], device_id=peer, device_id_type=MESH)

    def chain_ok(k):
        if k == 0 or k > 9:
            return None
        ok = L >= k
        return ok if k <= 8 else ok & (c == 1)

    def chain_send_ok(k):
        ok = (L >= k) & (L < 15)
        if k + 1 <= 8:
            return ok
        return ok & (c == 1) if k + 1 == 9 else None

    def yh_ok(k, to_h):
        ok = L >= k
        if k == 0:
            return ok & ~((c == 1) & (to_h == 0))
        if k == 9:
            return ok & (c == 1) & (to_h == 0)
        return ok

    def sib_ok(k, to_c):
        ok = L >= k
        if k == 0:
            return ok & (to_c == 1)
        if k == 9:
            return ok & (to_c == 0)
        return ok

    def diag_ok(k, to_c):
        ok = L >= k
        if k == 0:
            return ok & (to_c == 1)
        if k == 8:
            return ok & ~((to_c == 1) & (h == 1))
        if k == 9:
            return ok & (to_c == 0) & (h == 0)
        return ok

    def chain_out(k):
        return kv_copy(LAST - 4 * k, LAST - 4 * (k + 1), 0, k, chain_next)

    def yh_out(k):
        return kv_copy(LAST - 4 * k, LAST - 4 * k + 2 * h - 1, 1, k, yh_peer)

    def sib_out(k):
        return kv_copy(LAST - 4 * k, LAST - 4 * k + 4 * c - 2, 2, k, sib_peer)

    def diag_out(k):
        return kv_copy(LAST - 4 * k + 1 - 2 * h, LAST - 4 * k + 4 * c - 1 - 2 * h, 3, k, sib_peer)

    def arrived(slot):
        kv_copy(slot, slot, 0, 0, sib_peer).wait_recv()

    def when(cond, body):
        if cond is not None:
            pl.when(cond)(body)

    def step_chain(k):
        when(chain_ok(k), lambda: arrived(LAST - 4 * k))
        when(chain_send_ok(k), lambda: chain_out(k).start())
        has = L >= k if k <= 8 else (L >= k) & (c == 1)
        when(has & yh_ok(k, 1 - h), lambda: yh_out(k).start())
        when(has & sib_ok(k, 1 - c), lambda: sib_out(k).start())

    def step_yh(k):
        when(yh_ok(k, h), lambda: arrived(LAST - 4 * k + 1 - 2 * h))
        when(diag_ok(k, 1 - c), lambda: diag_out(k).start())

    def step_sib(k):
        when(sib_ok(k, c), lambda: arrived(LAST - 4 * k + 2 - 4 * c))
        when(diag_ok(k, c), lambda: arrived(LAST - 4 * k + 3 - 4 * c - 2 * h))

    lane = lax.broadcasted_iota(jnp.int32, (TOK, TOK), 1)
    sub = lax.broadcasted_iota(jnp.int32, (TOK, TOK), 0)
    eye = lane == sub

    def part(j, a, first, count):
        q = qbuf[j, pl.ds(a * TOK, TOK), :]
        k = kv[rows_of(first, count), 0:HD]
        v = kv[rows_of(first, count), HD:]
        v = jnp.concatenate([v, jnp.ones_like(v)], axis=1)
        s = lax.dot_general(q, k, (((1,), (1,)), ((), ())), preferred_element_type=jnp.float32)
        p = jnp.exp2(jnp.tanh(s * FACTOR) * GAIN)
        start = starts[j]
        tiles = []
        for t in range(count):
            slot = first + t
            key_pos = (4 * (u - LAST + slot) + x) * TOK + lane
            ok = key_pos >= start
            if slot == LAST:
                ok = ok & (key_pos <= (4 * u + (x + j) % 4) * TOK + sub)
            tiles.append(jnp.where(ok, p[:, t * TOK:(t + 1) * TOK], 0.0).astype(jnp.bfloat16))
        return jnp.dot(jnp.concatenate(tiles, axis=1), v, preferred_element_type=jnp.float32)

    def add(j, first, count, fresh=False):
        def one(a, carry):
            rows = pl.ds(a * TOK, TOK)
            new = part(j, a, first, count)
            acc[j, rows, :] = new if fresh else acc[j, rows, :] + new
            return carry
        lax.fori_loop(0, HEADS, one, 0)

    def give(j, total_of):
        def one(a, carry):
            total = total_of(a)
            osend[j - 1, pl.ds(a * TOK, TOK), :] = total[:, 0:HD].astype(jnp.bfloat16)
            dsend[j - 1, pl.ds(a, 1), :] = jnp.sum(jnp.where(eye, total[:, HD:], 0.0), axis=0, keepdims=True)
            return carry
        lax.fori_loop(0, HEADS, one, 0)
        o_copy(j).start()
        d_copy(j).start()

    R0, R1, R2, R3, R4 = (31, 4), (23, 8), (15, 8), (7, 8), (0, 7)

    step_chain(0)
    q_copy(1).start()
    q_copy(3).start()
    step_yh(0); step_chain(1); step_sib(0); step_yh(1); step_chain(2); step_sib(1)
    add(0, *R0, fresh=True)
    q_copy(2).start()
    step_yh(2); step_chain(3); step_sib(2); step_yh(3); step_chain(4); step_sib(3)
    add(0, *R1)
    step_yh(4); step_chain(5); step_sib(4)
    q_copy(1).wait_recv()
    add(1, *R0, fresh=True)
    step_yh(5); step_chain(6); step_sib(5)
    add(1, *R1)
    step_yh(6); step_chain(7); step_sib(6)
    add(0, *R2)
    step_yh(7); step_chain(8); step_sib(7)
    add(1, *R2)
    step_yh(8); step_chain(9); step_sib(8)
    add(1, *R3)
    step_yh(9); step_sib(9)
    give(1, lambda a: acc[1, pl.ds(a * TOK, TOK), :] + part(1, a, *R4))
    q_copy(3).wait_recv()
    give(3, lambda a: part(3, a, 0, LAST + 1))
    q_copy(2).wait_recv()
    give(2, lambda a: part(2, a, 0, LAST + 1))
    add(0, 0, 15)

    for j in (1, 3, 2):
        o_copy(j).wait_recv()
        d_copy(j).wait_recv()
    for a in range(HEADS):
        rows = slice(a * TOK, (a + 1) * TOK)
        num = acc[0, rows, 0:HD]
        den = drecv[0, a:a + 1, :] + drecv[1, a:a + 1, :] + drecv[2, a:a + 1, :]
        den = jnp.sum(jnp.where(eye, den, 0.0), axis=1, keepdims=True) + acc[0, rows, HD:]
        for j in range(3):
            num = num + orecv[j, rows, :].astype(jnp.float32)
        o_ref[:, a * HD:(a + 1) * HD] = (num / den).astype(jnp.bfloat16)

    for j in (1, 2, 3):
        q_copy(j).wait_send()
        o_copy(j).wait_send()
        d_copy(j).wait_send()
    for k in range(10):
        has = L >= k if k <= 8 else (L >= k) & (c == 1)
        when(chain_send_ok(k), lambda: chain_out(k).wait_send())
        when(has & yh_ok(k, 1 - h), lambda: yh_out(k).wait_send())
        when(has & sib_ok(k, 1 - c), lambda: sib_out(k).wait_send())
        when(diag_ok(k, 1 - c), lambda: diag_out(k).wait_send())


def per_device(queries, keys, values, doc_lengths):
    vmem = pl.BlockSpec(memory_space=pltpu.VMEM)
    return pl.pallas_call(
        kernel,
        out_shape=jax.ShapeDtypeStruct((TOK, HEADS * HD), jnp.bfloat16),
        in_specs=[vmem, vmem, vmem, pl.BlockSpec(memory_space=pltpu.SMEM)],
        out_specs=vmem,
        scratch_shapes=[
            pltpu.VMEM((SLOTS * TOK, 2 * HD), jnp.bfloat16),
            pltpu.VMEM((4, ROWS, HD), jnp.bfloat16),
            pltpu.VMEM((4, TOK, TOK), jnp.int32),
            pltpu.VMEM((2, ROWS, 2 * HD), jnp.float32),
            pltpu.VMEM((3, ROWS, HD), jnp.bfloat16),
            pltpu.VMEM((3, ROWS, HD), jnp.bfloat16),
            pltpu.VMEM((3, HEADS, TOK), jnp.float32),
            pltpu.VMEM((3, HEADS, TOK), jnp.float32),
            pltpu.SemaphoreType.DMA((SLOTS,)),
            pltpu.SemaphoreType.DMA((4, 10)),
            pltpu.SemaphoreType.DMA((3,)),
            pltpu.SemaphoreType.DMA((3,)),
            pltpu.SemaphoreType.DMA((3,)),
            pltpu.SemaphoreType.DMA((3,)),
            pltpu.SemaphoreType.DMA((3,)),
            pltpu.SemaphoreType.DMA((3,)),
        ],
        compiler_params=pltpu.CompilerParams(
            collective_id=0, has_side_effects=True, vmem_limit_bytes=48 * 1024 * 1024),
        name="packed_attention",
    )(queries, keys, values, doc_lengths)


def solution(mesh):
    return jax.shard_map(
        per_device,
        mesh=mesh,
        in_specs=(
            P(("ctx", "head"), None),
            P(("ctx", "head"), None),
            P(("ctx", "head"), None),
            P(),
        ),
        out_specs=P(("ctx", "head"), None),
        check_vma=False,
    )
```

```python
import functools
import math

import jax
import jax.numpy as jnp
from jax import lax
from jax.experimental import pallas as pl
from jax.experimental.pallas import tpu as pltpu
from jax.sharding import PartitionSpec as P

MESH = pl.DeviceIdType.MESH
HD = 128
HEADS = 8
TOK = 128
NDOCS = 16
ROWS = HEADS * TOK
FACTOR = 1.0 / (30.0 * math.sqrt(HD))
GAIN = 30.0 * math.log2(math.e)
PAD = 4
LAST = 34
SLOTS = PAD + LAST + 2


def rows_of(slot, count=1):
    first = (slot + PAD) * TOK
    if not isinstance(first, int):
        first = pl.multiple_of(first, TOK)
    return pl.ds(first, count * TOK)


def kernel(
    q_ref, k_ref, v_ref, len_ref, o_ref,
    lens, local, kv, qbuf, starts, acc, osend, orecv, dsend, drecv,
    kv_recv, kv_send, q_recv, q_send, o_recv, o_send, d_recv, d_send,
):
    ctx = lax.axis_index("ctx")
    head = lax.axis_index("head")
    L = ctx // 2
    z = L % 8
    c = ctx % 2
    h = head // 4
    x = head % 4
    w = 2 * c + h
    u = 4 * L + w

    yh_peer = (ctx, (1 - h) * 4 + x)
    sib_peer = (L * 2 + 1 - c, head)

    def x_peer(j):
        return (ctx, h * 4 + (x + j) % 4)

    loads = [
        pltpu.make_async_copy(k_ref, kv.at[rows_of(LAST), pl.ds(0, HD)], local.at[0]),
        pltpu.make_async_copy(v_ref, kv.at[rows_of(LAST), pl.ds(HD, HD)], local.at[1]),
        pltpu.make_async_copy(len_ref, lens, local.at[2]),
    ] + [
        pltpu.make_async_copy(
            q_ref.at[:, pl.ds(a * HD, HD)], qbuf.at[0, pl.ds(a * TOK, TOK)], local.at[3 + a])
        for a in range(HEADS)
    ]
    for load in loads:
        load.start()
    kv[0:(PAD + LAST) * TOK, :] = jnp.zeros(((PAD + LAST) * TOK, 2 * HD), kv.dtype)
    kv[(PAD + LAST + 1) * TOK:, :] = jnp.zeros((TOK, 2 * HD), kv.dtype)

    barrier = pltpu.get_barrier_semaphore()
    for peer in (yh_peer, sib_peer, x_peer(1), x_peer(2), x_peer(3)):
        pl.semaphore_signal(barrier, inc=1, device_id=peer, device_id_type=MESH)

    links = [(L < 15, 1), (L > 0, -1), (L < 8, 8), (L > 7, -8)]
    for k in (5, 6, 7):
        links += [(z + k < 8, k), (z >= k, -k)]
    count = jnp.int32(5)
    for ok, away in links:
        count = count + ok.astype(jnp.int32)

        @pl.when(ok)
        def _():
            pl.semaphore_signal(
                barrier, inc=1, device_id=(ctx + 2 * away, head), device_id_type=MESH)

    for load in loads:
        load.wait()

    for j in range(4):
        pos = (4 * u + (x + j) % 4) * TOK + lax.broadcasted_iota(jnp.int32, (TOK, TOK), 0)
        end = jnp.int32(0)
        start = jnp.zeros((TOK, TOK), jnp.int32)
        for d in range(NDOCS):
            length = lens[d]
            end = end + length
            start = start + jnp.where(pos >= end, length, 0)
        starts[j] = start

    pl.semaphore_wait(barrier, count)

    def q_copy(j):
        return pltpu.make_async_remote_copy(
            src_ref=qbuf.at[0], dst_ref=qbuf.at[j], send_sem=q_send.at[j - 1],
            recv_sem=q_recv.at[j - 1], device_id=x_peer(4 - j), device_id_type=MESH)

    def o_copy(j):
        return pltpu.make_async_remote_copy(
            src_ref=osend.at[j - 1], dst_ref=orecv.at[j - 1], send_sem=o_send.at[j - 1],
            recv_sem=o_recv.at[j - 1], device_id=x_peer(j), device_id_type=MESH)

    def d_copy(j):
        return pltpu.make_async_remote_copy(
            src_ref=dsend.at[j - 1], dst_ref=drecv.at[j - 1], send_sem=d_send.at[j - 1],
            recv_sem=d_recv.at[j - 1], device_id=x_peer(j), device_id_type=MESH)

    def kv_copy(src, dst, kind, k, peer):
        return pltpu.make_async_remote_copy(
            src_ref=kv.at[rows_of(src)], dst_ref=kv.at[rows_of(dst)], send_sem=kv_send.at[kind, k],
            recv_sem=kv_recv.at[dst + PAD], device_id=peer, device_id_type=MESH)

    def owned(k):
        return L >= k if k <= 8 else (L >= k) & (c == 1)

    def out(k, to_k, away, kind, at):
        return kv_copy(LAST - 4 * k, LAST - 4 * to_k, kind, at, (ctx + 2 * away, head))

    def chain_sends(k):
        sends = []
        if k <= 3:
            sends.append(((L >= k) & (L < 15), out(k, k + 1, 1, 0, k)))
        if k == 0:
            sends.append((L < 8, out(0, 8, 8, 0, 8)))
            for far in (5, 6, 7):
                sends.append((z + far < 8, out(0, far, far, 0, far)))
        if 6 <= k <= 8:
            sends.append(((L >= 9) & (L - k < 8) & (L >= k), out(k, k - 1, -1, 0, 9 if k == 6 else k + 3)))
        if k == 8:
            sends.append(((L >= 8) & (L < 15) & (c == 1), out(8, 9, 1, 0, 4)))
        return sends

    def yh_ok(k, to_h):
        ok = L >= k
        if k == 0:
            return ok & ~((c == 1) & (to_h == 0))
        if k == 9:
            return ok & (c == 1) & (to_h == 0)
        return ok

    def sib_ok(k, to_c):
        ok = L >= k
        if k == 0:
            return ok & (to_c == 1)
        if k == 9:
            return ok & (to_c == 0)
        return ok

    def diag_ok(k, to_c):
        ok = L >= k
        if k == 0:
            return ok & (to_c == 1)
        if k == 8:
            return ok & ~((to_c == 1) & (h == 1))
        if k == 9:
            return ok & (to_c == 0) & (h == 0)
        return ok

    def yh_out(k):
        return kv_copy(LAST - 4 * k, LAST - 4 * k + 2 * h - 1, 1, k, yh_peer)

    def sib_out(k):
        return kv_copy(LAST - 4 * k, LAST - 4 * k + 4 * c - 2, 2, k, sib_peer)

    def diag_out(k):
        return kv_copy(LAST - 4 * k + 1 - 2 * h, LAST - 4 * k + 4 * c - 1 - 2 * h, 3, k, sib_peer)

    def arrived(slot):
        kv_copy(slot, slot, 0, 0, sib_peer).wait_recv()

    def when(cond, body):
        if cond is not None:
            pl.when(cond)(body)

    def step_chain(k):
        if k:
            when(owned(k), lambda: arrived(LAST - 4 * k))
        for ok, copy in chain_sends(k):
            when(ok, copy.start)
        when(owned(k) & yh_ok(k, 1 - h), lambda: yh_out(k).start())
        when(owned(k) & sib_ok(k, 1 - c), lambda: sib_out(k).start())

    def step_yh(k):
        when(yh_ok(k, h), lambda: arrived(LAST - 4 * k + 1 - 2 * h))
        when(diag_ok(k, 1 - c), lambda: diag_out(k).start())

    def step_sib(k):
        when(sib_ok(k, c), lambda: arrived(LAST - 4 * k + 2 - 4 * c))
        when(diag_ok(k, c), lambda: arrived(LAST - 4 * k + 3 - 4 * c - 2 * h))

    lane = lax.broadcasted_iota(jnp.int32, (TOK, TOK), 1)
    sub = lax.broadcasted_iota(jnp.int32, (TOK, TOK), 0)
    eye = lane == sub

    def part(j, a, first, count):
        q = qbuf[j, pl.ds(a * TOK, TOK), :]
        k = kv[rows_of(first, count), 0:HD]
        v = kv[rows_of(first, count), HD:]
        v = jnp.concatenate([v, jnp.ones_like(v)], axis=1)
        s = lax.dot_general(q, k, (((1,), (1,)), ((), ())), preferred_element_type=jnp.float32)
        p = jnp.exp2(jnp.tanh(s * FACTOR) * GAIN)
        start = starts[j]
        tiles = []
        for t in range(count):
            slot = first + t
            key_pos = (4 * (u - LAST + slot) + x) * TOK + lane
            ok = key_pos >= start
            if slot == LAST:
                ok = ok & (key_pos <= (4 * u + (x + j) % 4) * TOK + sub)
            tiles.append(jnp.where(ok, p[:, t * TOK:(t + 1) * TOK], 0.0).astype(jnp.bfloat16))
        return jnp.dot(jnp.concatenate(tiles, axis=1), v, preferred_element_type=jnp.float32)

    def add(j, first, count, fresh=False):
        def one(a, carry):
            rows = pl.ds(a * TOK, TOK)
            new = part(j, a, first, count)
            acc[j, rows, :] = new if fresh else acc[j, rows, :] + new
            return carry
        lax.fori_loop(0, HEADS, one, 0, unroll=True)

    def give(j, total_of):
        def one(a, carry):
            total = total_of(a)
            osend[j - 1, pl.ds(a * TOK, TOK), :] = total[:, 0:HD].astype(jnp.bfloat16)
            dsend[j - 1, pl.ds(a, 1), :] = jnp.sum(jnp.where(eye, total[:, HD:], 0.0), axis=0, keepdims=True)
            return carry
        lax.fori_loop(0, HEADS, one, 0, unroll=True)
        o_copy(j).start()
        d_copy(j).start()

    step_chain(0)
    q_copy(1).start()
    q_copy(3).start()
    step_chain(8)
    step_chain(1)
    step_yh(0)
    step_chain(7)
    step_chain(9)
    step_chain(2)
    step_yh(8)
    step_yh(1)
    step_sib(0)
    step_sib(1)
    add(0, 30, 5, fresh=True)
    q_copy(2).start()
    step_chain(6)
    step_chain(3)
    step_yh(9)
    step_yh(7)
    step_yh(2)
    for k in (8, 9, 7, 2):
        step_sib(k)
    add(0, 26, 4)
    step_chain(5)
    step_chain(4)
    step_yh(6)
    step_yh(3)
    add(0, 0, 7)
    step_yh(5)
    step_yh(4)
    q_copy(1).wait_recv()
    add(1, 26, 9, fresh=True)
    add(1, 0, 7)
    for k in (6, 3, 5, 4):
        step_sib(k)
    give(1, lambda a: acc[1, pl.ds(a * TOK, TOK), :] + part(1, a, 7, 19))

    def whole(i, carry):
        j = 3 - i
        q_copy(j).wait_recv()
        give(j, lambda a: part(j, a, 0, LAST + 1))
        return carry

    lax.fori_loop(0, 2, whole, 0)
    add(0, 7, 19)

    for j in (1, 3, 2):
        o_copy(j).wait_recv()
        d_copy(j).wait_recv()
    for a in range(HEADS):
        rows = slice(a * TOK, (a + 1) * TOK)
        num = acc[0, rows, 0:HD]
        den = drecv[0, a:a + 1, :] + drecv[1, a:a + 1, :] + drecv[2, a:a + 1, :]
        den = jnp.sum(jnp.where(eye, den, 0.0), axis=1, keepdims=True) + acc[0, rows, HD:]
        for j in range(3):
            num = num + orecv[j, rows, :].astype(jnp.float32)
        o_ref[:, a * HD:(a + 1) * HD] = (num / den).astype(jnp.bfloat16)

    for j in (1, 2, 3):
        q_copy(j).wait_send()
        o_copy(j).wait_send()
        d_copy(j).wait_send()
    for k in range(10):
        for ok, copy in chain_sends(k):
            when(ok, copy.wait_send)
        when(owned(k) & yh_ok(k, 1 - h), lambda: yh_out(k).wait_send())
        when(owned(k) & sib_ok(k, 1 - c), lambda: sib_out(k).wait_send())
        when(diag_ok(k, 1 - c), lambda: diag_out(k).wait_send())


def per_device(queries, keys, values, doc_lengths):
    return pl.pallas_call(
        kernel,
        out_shape=jax.ShapeDtypeStruct((TOK, HEADS * HD), jnp.bfloat16),
        in_specs=[pl.BlockSpec(memory_space=pl.ANY)] * 4,
        out_specs=pl.BlockSpec(memory_space=pltpu.VMEM),
        scratch_shapes=[
            pltpu.SMEM((NDOCS,), jnp.int32),
            pltpu.SemaphoreType.DMA((3 + HEADS,)),
            pltpu.VMEM((SLOTS * TOK, 2 * HD), jnp.bfloat16),
            pltpu.VMEM((4, ROWS, HD), jnp.bfloat16),
            pltpu.VMEM((4, TOK, TOK), jnp.int32),
            pltpu.VMEM((2, ROWS, 2 * HD), jnp.float32),
            pltpu.VMEM((3, ROWS, HD), jnp.bfloat16),
            pltpu.VMEM((3, ROWS, HD), jnp.bfloat16),
            pltpu.VMEM((3, HEADS, TOK), jnp.float32),
            pltpu.VMEM((3, HEADS, TOK), jnp.float32),
            pltpu.SemaphoreType.DMA((SLOTS,)),
            pltpu.SemaphoreType.DMA((4, 12)),
            pltpu.SemaphoreType.DMA((3,)),
            pltpu.SemaphoreType.DMA((3,)),
            pltpu.SemaphoreType.DMA((3,)),
            pltpu.SemaphoreType.DMA((3,)),
            pltpu.SemaphoreType.DMA((3,)),
            pltpu.SemaphoreType.DMA((3,)),
        ],
        compiler_params=pltpu.CompilerParams(
            collective_id=0, has_side_effects=True, vmem_limit_bytes=60 * 1024 * 1024),
        name="packed_attention",
    )(queries, keys, values, doc_lengths)


def solution(mesh):
    return jax.shard_map(
        per_device,
        mesh=mesh,
        in_specs=(
            P(("ctx", "head"), None),
            P(("ctx", "head"), None),
            P(("ctx", "head"), None),
            P(),
        ),
        out_specs=P(("ctx", "head"), None),
        check_vma=False,
    )
```

```python
import functools
import math

import jax
import jax.numpy as jnp
from jax import lax
from jax.experimental import pallas as pl
from jax.experimental.pallas import tpu as pltpu
from jax.sharding import PartitionSpec as P

MESH = pl.DeviceIdType.MESH
HD = 128
HEADS = 8
TOK = 128
NDOCS = 16
ROWS = HEADS * TOK
FACTOR = 1.0 / (30.0 * math.sqrt(HD))
GAIN = 30.0 * math.log2(math.e)
OWN, SIB, YH, DIAG = range(4)
ACROSS = (1, 8)
ORDER = (0, 1, 8, 2, 7, 3, 6, 4, 5)
EARLY = [(g, p) for g in (OWN, SIB) for p in (0, 1, 2)] + [(g, p) for g in (OWN, SIB) for p in (3, 4)]
EARLY += [(g, p) for g in (YH, DIAG) for p in (0, 1, 2)] + [(g, p) for g in (YH, DIAG) for p in (3, 4)]
LATE = [(g, p) for g in (OWN, SIB, YH, DIAG) for p in (5, 6)]
LATE += [(g, p) for g in (OWN, SIB, YH, DIAG) for p in (7, 8)]
SLOT = EARLY + LATE + [(OWN, 9), (YH, 9)]


def place(g, k):
    if k == 9:
        return SLOT.index((g, 9 if g in (OWN, YH) else 0))
    return SLOT.index((g, ORDER.index(k)))


def rows_of(slot, count=1):
    return pl.ds(slot * TOK, count * TOK)


def kernel(
    q_ref, k_ref, v_ref, len_ref, o_ref,
    lens, local, kv, qbuf, starts, acc, osend, orecv, dsend, drecv,
    kv_recv, kv_send, q_recv, q_send, o_recv, o_send, d_recv, d_send,
):
    ctx = lax.axis_index("ctx")
    head = lax.axis_index("head")
    L = ctx // 2
    z = L % 8
    c = ctx % 2
    h = head // 4
    x = head % 4
    w = 2 * c + h
    u = 4 * L + w

    other = (1 - h) * 4 + x
    yh_peer = (ctx, other)
    sib_peer = (L * 2 + 1 - c, head)

    def x_peer(j):
        return (ctx, h * 4 + (x + j) % 4)

    barrier = pltpu.get_barrier_semaphore()
    for peer in (yh_peer, sib_peer, x_peer(1), x_peer(2), x_peer(3)):
        pl.semaphore_signal(barrier, inc=1, device_id=peer, device_id_type=MESH)

    count = jnp.int32(5)
    for away in range(1, 10):
        from_ok, to_ok = L >= away, L + away < 16
        if away == 9:
            from_ok, to_ok = from_ok & (c == 1), to_ok & (c == 1)
        peers = [head] * (away not in (3, 4)) + [other] * (away in ACROSS)
        count = count + len(peers) * to_ok.astype(jnp.int32)

        @pl.when(from_ok)
        def _():
            for peer in peers:
                pl.semaphore_signal(
                    barrier, inc=1, device_id=(ctx - 2 * away, peer), device_id_type=MESH)

    loads = [
        pltpu.make_async_copy(k_ref, kv.at[rows_of(0), pl.ds(0, HD)], local.at[0]),
        pltpu.make_async_copy(v_ref, kv.at[rows_of(0), pl.ds(HD, HD)], local.at[1]),
        pltpu.make_async_copy(len_ref, lens, local.at[2]),
    ] + [
        pltpu.make_async_copy(
            q_ref.at[:, pl.ds(a * HD, HD)], qbuf.at[0, pl.ds(a * TOK, TOK)], local.at[3 + a])
        for a in range(HEADS)
    ]
    for load in loads:
        load.start()

    for slot, (g, p) in enumerate(EARLY + LATE):
        empty = L < ORDER[p]
        if p == 0 and g == SIB:
            empty = (c == 0) & (L < 9)
        if p == 0 and g == DIAG:
            empty = (c == 0) & ((L < 9) | (h == 1))
        if p == 0 and g in (OWN, YH):
            continue

        @pl.when(empty)
        def _():
            kv[rows_of(slot), :] = jnp.zeros((TOK, 2 * HD), kv.dtype)

    for load in loads:
        load.wait()

    pl.semaphore_wait(barrier, count)

    def q_copy(j):
        return pltpu.make_async_remote_copy(
            src_ref=qbuf.at[0], dst_ref=qbuf.at[j], send_sem=q_send.at[j - 1],
            recv_sem=q_recv.at[j - 1], device_id=x_peer(4 - j), device_id_type=MESH)

    def o_copy(j, half):
        rows = pl.ds(half * (ROWS // 2), ROWS // 2)
        return pltpu.make_async_remote_copy(
            src_ref=osend.at[j - 1, rows], dst_ref=orecv.at[j - 1, rows], send_sem=o_send.at[j - 1, half],
            recv_sem=o_recv.at[j - 1, half], device_id=x_peer(j if j != 2 else 1 + 2 * half),
            device_id_type=MESH)

    def d_copy(j):
        return pltpu.make_async_remote_copy(
            src_ref=dsend.at[j - 1], dst_ref=drecv.at[j - 1], send_sem=d_send.at[j - 1],
            recv_sem=d_recv.at[j - 1], device_id=x_peer(j), device_id_type=MESH)

    def kv_copy(src, dst, kind, k, peer):
        return pltpu.make_async_remote_copy(
            src_ref=kv.at[rows_of(src)], dst_ref=kv.at[rows_of(dst)], send_sem=kv_send.at[kind, k],
            recv_sem=kv_recv.at[dst], device_id=peer, device_id_type=MESH)

    def owned(k):
        return L >= k if k <= 8 else (L >= k) & (c == 1)

    def out(k, to_k, across=False):
        return kv_copy(
            place(OWN, k), place(YH if across else OWN, to_k), 1 if across else 0, to_k,
            (ctx + 2 * (to_k - k), other if across else head))

    def first_sends():
        sends = [(L + 1 < 16, out(0, 1)), (L + 8 < 16, out(0, 8))]
        sends += [(L + 1 < 16, out(0, 1, True)), (L + 8 < 16, out(0, 8, True))]
        sends += [(L + 2 < 16, out(0, 2)), (L + 7 < 16, out(0, 7)), ((L + 9 < 16) & (c == 1), out(0, 9))]
        return sends

    def second_sends():
        return [(L + 6 < 16, out(0, 6)), (L + 5 < 16, out(0, 5))]

    def third_sends():
        return [((L >= 2) & (L + 1 < 16), out(2, 3)), ((L >= 2) & (L + 2 < 16), out(2, 4))]

    def yh_ok(k, to_h):
        return L >= k if k <= 8 else (L >= k) & (c == 1) & (to_h == 0)

    def sib_ok(k, to_c):
        if k in (0, 9):
            return (L >= k) & (to_c == (0 if k else 1))
        return L >= k

    def diag_ok(k, to_c):
        if k == 0:
            return to_c == 1
        return L >= k if k <= 8 else (L >= k) & (to_c == 0) & (h == 0)

    def yh_out(k):
        return kv_copy(place(OWN, k), place(YH, k), 1, k, yh_peer)

    def sib_out(k):
        return kv_copy(place(OWN, k), place(SIB, k), 2, k, sib_peer)

    def diag_out(k):
        return kv_copy(place(YH, k), place(DIAG, k), 3, k, sib_peer)

    def arrived(slot):
        kv_copy(slot, slot, 0, 0, sib_peer).wait_recv()

    def send(sends):
        for ok, copy in sends:
            pl.when(ok)(copy.start)

    def step_own(k):
        if k:
            pl.when(owned(k))(lambda: arrived(place(OWN, k)))
        if k == 2:
            send(third_sends())
        if k not in ACROSS:
            pl.when(owned(k) & yh_ok(k, 1 - h))(lambda: yh_out(k).start())
        pl.when(owned(k) & sib_ok(k, 1 - c))(lambda: sib_out(k).start())

    def step_yh(k):
        pl.when(yh_ok(k, h))(lambda: arrived(place(YH, k)))
        pl.when(diag_ok(k, 1 - c))(lambda: diag_out(k).start())

    def step_sib(*ks):
        for k in ks:
            pl.when(sib_ok(k, c))(lambda: arrived(place(SIB, k)))

    def step_diag(*ks):
        for k in ks:
            pl.when(diag_ok(k, c))(lambda: arrived(place(DIAG, k)))

    lane = lax.broadcasted_iota(jnp.int32, (TOK, TOK), 1)
    sub = lax.broadcasted_iota(jnp.int32, (TOK, TOK), 0)
    eye = lane == sub

    def part(j, a, first, count):
        q = qbuf[j, pl.ds(a * TOK, TOK), :]
        k = kv[rows_of(first, count), 0:HD]
        v = kv[rows_of(first, count), HD:]
        v = jnp.concatenate([v, jnp.ones_like(v)], axis=1)
        s = lax.dot_general(q, k, (((1,), (1,)), ((), ())), preferred_element_type=jnp.float32)
        p = jnp.exp2(jnp.tanh(s * FACTOR) * GAIN)
        start = starts[j]
        tiles = []
        for t in range(count):
            g, at = SLOT[first + t]
            k_of = 9 * (1 - c) if at == 0 and g in (SIB, DIAG) else ORDER[at]
            w_of = w + (1 - 2 * h if g in (YH, DIAG) else 0) + (2 - 4 * c if g in (SIB, DIAG) else 0)
            key_pos = (4 * (4 * (L - k_of) + w_of) + x) * TOK + lane
            ok = key_pos >= start
            if at == 0:
                ok = ok & (key_pos <= (4 * u + (x + j) % 4) * TOK + sub)
            tiles.append(jnp.where(ok, p[:, t * TOK:(t + 1) * TOK], 0.0).astype(jnp.bfloat16))
        return jnp.dot(jnp.concatenate(tiles, axis=1), v, preferred_element_type=jnp.float32)

    def add(j, first, count, fresh=False, heads=(0, HEADS)):
        def one(a, carry):
            rows = pl.ds(a * TOK, TOK)
            new = part(j, a, first, count)
            acc[j, rows, :] = new if fresh else acc[j, rows, :] + new
            return carry
        lax.fori_loop(*heads, one, 0, unroll=True)

    def give(j, half, first=None, count=0, passing=False):
        def one(a, carry):
            rows = pl.ds(a * TOK, TOK)
            total = acc[j, rows, :]
            if count:
                total = total + part(j, a, first, count)
            numerator = total[:, 0:HD]
            if passing:
                numerator = numerator + orecv[1, rows, :].astype(jnp.float32)
            osend[j - 1, rows, :] = numerator.astype(jnp.bfloat16)
            dsend[j - 1, pl.ds(a, 1), :] = jnp.sum(jnp.where(eye, total[:, HD:], 0.0), axis=0, keepdims=True)
            return carry
        lax.fori_loop(half * HEADS // 2, (half + 1) * HEADS // 2, one, 0, unroll=True)
        o_copy(j, half).start()

    def others(first, count, hooks, fresh=False):
        def one(i, carry):
            j = 1 + (2 * i) % 3
            if fresh:
                q_copy(j).wait_recv()
            add(j, first, count, fresh)
            for at, hook in enumerate(hooks):
                pl.when(i == at)(hook)
            return carry
        lax.fori_loop(0, 3, one, 0)

    def steps(*pairs):
        def run():
            for step, k in pairs:
                step(k)
        return run

    send(first_sends())
    step_own(0)
    q_copy(1).start()
    q_copy(3).start()

    for j in range(4):
        pos = (4 * u + (x + j) % 4) * TOK + lax.broadcasted_iota(jnp.int32, (TOK, TOK), 0)
        end = jnp.int32(0)
        start = jnp.zeros((TOK, TOK), jnp.int32)
        for d in range(NDOCS):
            length = lens[d]
            end = end + length
            start = start + jnp.where(pos >= end, length, 0)
        starts[j] = start

    step_own(1)
    step_own(8)
    step_sib(0, 1, 8)
    step_own(9)
    step_sib(9)
    add(0, 0, 6, fresh=True)
    q_copy(2).start()
    step_yh(0)
    step_yh(1)
    step_yh(8)
    step_own(2)
    step_own(7)
    send(second_sends())
    step_sib(2, 7)
    add(0, 6, 4)
    others(0, 10, [
        steps((step_yh, 9), (step_yh, 2), (step_yh, 7)),
        steps((step_own, 3), (step_own, 6)),
        steps((step_diag, 0), (step_diag, 1), (step_diag, 8), (step_diag, 9), (step_diag, 2), (step_diag, 7)),
    ], fresh=True)
    others(10, 10, [
        steps((step_own, 5), (step_own, 4)),
        steps((step_yh, 3), (step_yh, 6)),
        steps((step_sib, 3), (step_sib, 6), (step_diag, 3), (step_diag, 6)),
    ])
    others(20, 8, [
        steps((step_yh, 5), (step_yh, 4)),
        steps(),
        steps((step_sib, 4), (step_sib, 5), (step_diag, 4), (step_diag, 5)),
    ])

    give(2, 0, 28, 8)
    give(2, 1, 28, 8)
    d_copy(2).start()
    give(1, 1, 28, 8)
    give(3, 0, 28, 8)
    add(1, 28, 8, heads=(0, HEADS // 2))
    add(3, 28, 8, heads=(HEADS // 2, HEADS))
    add(0, 10, 10)
    o_copy(2, 0).wait_recv()
    give(1, 0, passing=True)
    o_copy(2, 1).wait_recv()
    give(3, 1, passing=True)
    d_copy(1).start()
    d_copy(3).start()
    add(0, 20, 16)

    for j in (2, 3, 1):
        d_copy(j).wait_recv()
    for a in range(HEADS):
        if a % (HEADS // 2) == 0:
            for j in (1, 3):
                o_copy(j, a // (HEADS // 2)).wait_recv()
        rows = slice(a * TOK, (a + 1) * TOK)
        num = acc[0, rows, 0:HD]
        den = drecv[0, a:a + 1, :] + drecv[1, a:a + 1, :] + drecv[2, a:a + 1, :]
        den = jnp.sum(jnp.where(eye, den, 0.0), axis=1, keepdims=True) + acc[0, rows, HD:]
        for j in (0, 2):
            num = num + orecv[j, rows, :].astype(jnp.float32)
        o_ref[:, a * HD:(a + 1) * HD] = (num / den).astype(jnp.bfloat16)

    for j in (1, 2, 3):
        q_copy(j).wait_send()
        o_copy(j, 0).wait_send()
        o_copy(j, 1).wait_send()
        d_copy(j).wait_send()
    for ok, copy in first_sends() + second_sends() + third_sends():
        pl.when(ok)(copy.wait_send)
    for k in range(10):
        if k not in ACROSS:
            pl.when(owned(k) & yh_ok(k, 1 - h))(lambda: yh_out(k).wait_send())
        pl.when(owned(k) & sib_ok(k, 1 - c))(lambda: sib_out(k).wait_send())
        pl.when(diag_ok(k, 1 - c))(lambda: diag_out(k).wait_send())


def per_device(queries, keys, values, doc_lengths):
    return pl.pallas_call(
        kernel,
        out_shape=jax.ShapeDtypeStruct((TOK, HEADS * HD), jnp.bfloat16),
        in_specs=[pl.BlockSpec(memory_space=pl.ANY)] * 4,
        out_specs=pl.BlockSpec(memory_space=pltpu.VMEM),
        scratch_shapes=[
            pltpu.SMEM((NDOCS,), jnp.int32),
            pltpu.SemaphoreType.DMA((3 + HEADS,)),
            pltpu.VMEM((len(SLOT) * TOK, 2 * HD), jnp.bfloat16),
            pltpu.VMEM((4, ROWS, HD), jnp.bfloat16),
            pltpu.VMEM((4, TOK, TOK), jnp.int32),
            pltpu.VMEM((4, ROWS, 2 * HD), jnp.float32),
            pltpu.VMEM((3, ROWS, HD), jnp.bfloat16),
            pltpu.VMEM((3, ROWS, HD), jnp.bfloat16),
            pltpu.VMEM((3, HEADS, TOK), jnp.float32),
            pltpu.VMEM((3, HEADS, TOK), jnp.float32),
            pltpu.SemaphoreType.DMA((len(SLOT),)),
            pltpu.SemaphoreType.DMA((4, 10)),
            pltpu.SemaphoreType.DMA((3,)),
            pltpu.SemaphoreType.DMA((3,)),
            pltpu.SemaphoreType.DMA((3, 2)),
            pltpu.SemaphoreType.DMA((3, 2)),
            pltpu.SemaphoreType.DMA((3,)),
            pltpu.SemaphoreType.DMA((3,)),
        ],
        compiler_params=pltpu.CompilerParams(
            collective_id=0, has_side_effects=True, vmem_limit_bytes=40 * 1024 * 1024),
        name="packed_attention",
    )(queries, keys, values, doc_lengths)


def solution(mesh):
    return jax.shard_map(
        per_device,
        mesh=mesh,
        in_specs=(
            P(("ctx", "head"), None),
            P(("ctx", "head"), None),
            P(("ctx", "head"), None),
            P(),
        ),
        out_specs=P(("ctx", "head"), None),
        check_vma=False,
    )
```

```python
import functools
import math

import jax
import jax.numpy as jnp
from jax import lax
from jax.experimental import pallas as pl
from jax.experimental.pallas import tpu as pltpu
from jax.sharding import PartitionSpec as P

MESH = pl.DeviceIdType.MESH
HD = 128
HEADS = 8
TOK = 128
NDOCS = 16
ROWS = HEADS * TOK
FACTOR = 1.0 / (30.0 * math.sqrt(HD))
GAIN = 30.0 * math.log2(math.e)
OWN, SIB, YH, DIAG = range(4)
ACROSS = (1, 8)
ORDER = (0, 1, 8, 2, 7, 3, 6, 4, 5)
EARLY = [(g, p) for g in (OWN, SIB) for p in (0, 1, 2)] + [(g, p) for g in (OWN, SIB) for p in (3, 4)]
EARLY += [(g, p) for g in (YH, DIAG) for p in (0, 1, 2)] + [(g, p) for g in (YH, DIAG) for p in (3, 4)]
LATE = [(g, p) for g in (OWN, SIB, YH, DIAG) for p in (5, 6)]
LATE += [(g, p) for g in (OWN, SIB, YH, DIAG) for p in (7, 8)]
SLOT = EARLY + LATE + [(OWN, 9), (YH, 9)]


def place(g, k):
    if k == 9:
        return SLOT.index((g, 9 if g in (OWN, YH) else 0))
    return SLOT.index((g, ORDER.index(k)))


def rows_of(slot, count=1):
    return pl.ds(slot * TOK, count * TOK)


def kernel(
    q_ref, k_ref, v_ref, len_ref, o_ref,
    lens, local, kv, qbuf, starts, acc, osend, orecv, dsend, drecv,
    kv_recv, kv_send, q_recv, q_send, o_recv, o_send, d_recv, d_send,
):
    ctx = lax.axis_index("ctx")
    head = lax.axis_index("head")
    L = ctx // 2
    z = L % 8
    c = ctx % 2
    h = head // 4
    x = head % 4
    w = 2 * c + h
    u = 4 * L + w

    other = (1 - h) * 4 + x
    yh_peer = (ctx, other)
    sib_peer = (L * 2 + 1 - c, head)

    def x_peer(j):
        return (ctx, h * 4 + (x + j) % 4)

    barrier = pltpu.get_barrier_semaphore()
    for peer in (yh_peer, sib_peer, x_peer(1), x_peer(2), x_peer(3)):
        pl.semaphore_signal(barrier, inc=1, device_id=peer, device_id_type=MESH)

    count = jnp.int32(5)
    for away in range(1, 10):
        from_ok, to_ok = L >= away, L + away < 16
        if away == 9:
            from_ok, to_ok = from_ok & (c == 1), to_ok & (c == 1)
        peers = [head] * (away not in (3, 4)) + [other] * (away in ACROSS)
        count = count + len(peers) * to_ok.astype(jnp.int32)

        @pl.when(from_ok)
        def _():
            for peer in peers:
                pl.semaphore_signal(
                    barrier, inc=1, device_id=(ctx - 2 * away, peer), device_id_type=MESH)

    loads = [
        pltpu.make_async_copy(k_ref, kv.at[rows_of(0), pl.ds(0, HD)], local.at[0]),
        pltpu.make_async_copy(v_ref, kv.at[rows_of(0), pl.ds(HD, HD)], local.at[1]),
        pltpu.make_async_copy(len_ref, lens, local.at[2]),
    ] + [
        pltpu.make_async_copy(
            q_ref.at[:, pl.ds(a * HD, HD)], qbuf.at[0, pl.ds(a * TOK, TOK)], local.at[3 + a])
        for a in range(HEADS)
    ]
    for load in loads:
        load.start()

    for slot, (g, p) in enumerate(EARLY + LATE):
        empty = L < ORDER[p]
        if p == 0 and g == SIB:
            empty = (c == 0) & (L < 9)
        if p == 0 and g == DIAG:
            empty = (c == 0) & ((L < 9) | (h == 1))
        if p == 0 and g in (OWN, YH):
            continue

        @pl.when(empty)
        def _():
            kv[rows_of(slot), :] = jnp.zeros((TOK, 2 * HD), kv.dtype)

    for load in loads:
        load.wait()

    pl.semaphore_wait(barrier, count)

    def q_copy(j):
        return pltpu.make_async_remote_copy(
            src_ref=qbuf.at[0], dst_ref=qbuf.at[j], send_sem=q_send.at[j - 1],
            recv_sem=q_recv.at[j - 1], device_id=x_peer(4 - j), device_id_type=MESH)

    def o_copy(j, half):
        rows = pl.ds(half * (ROWS // 2), ROWS // 2)
        return pltpu.make_async_remote_copy(
            src_ref=osend.at[j - 1, rows], dst_ref=orecv.at[j - 1, rows], send_sem=o_send.at[j - 1, half],
            recv_sem=o_recv.at[j - 1, half], device_id=x_peer(j if j != 2 else 1 + 2 * half),
            device_id_type=MESH)

    def d_copy(j):
        return pltpu.make_async_remote_copy(
            src_ref=dsend.at[j - 1], dst_ref=drecv.at[j - 1], send_sem=d_send.at[j - 1],
            recv_sem=d_recv.at[j - 1], device_id=x_peer(j), device_id_type=MESH)

    def kv_copy(src, dst, kind, k, peer):
        return pltpu.make_async_remote_copy(
            src_ref=kv.at[rows_of(src)], dst_ref=kv.at[rows_of(dst)], send_sem=kv_send.at[kind, k],
            recv_sem=kv_recv.at[dst], device_id=peer, device_id_type=MESH)

    def owned(k):
        return L >= k if k <= 8 else (L >= k) & (c == 1)

    def out(k, to_k, across=False):
        return kv_copy(
            place(OWN, k), place(YH if across else OWN, to_k), 1 if across else 0, to_k,
            (ctx + 2 * (to_k - k), other if across else head))

    def first_sends():
        sends = [(L + 1 < 16, out(0, 1)), (L + 8 < 16, out(0, 8))]
        sends += [(L + 1 < 16, out(0, 1, True)), (L + 8 < 16, out(0, 8, True))]
        sends += [(L + 2 < 16, out(0, 2)), (L + 7 < 16, out(0, 7)), ((L + 9 < 16) & (c == 1), out(0, 9))]
        return sends

    def second_sends():
        return [(L + 6 < 16, out(0, 6)), (L + 5 < 16, out(0, 5))]

    def third_sends():
        return [((L >= 2) & (L + 1 < 16), out(2, 3)), ((L >= 2) & (L + 2 < 16), out(2, 4))]

    def yh_ok(k, to_h):
        return L >= k if k <= 8 else (L >= k) & (c == 1) & (to_h == 0)

    def sib_ok(k, to_c):
        if k in (0, 9):
            return (L >= k) & (to_c == (0 if k else 1))
        return L >= k

    def diag_ok(k, to_c):
        if k == 0:
            return to_c == 1
        return L >= k if k <= 8 else (L >= k) & (to_c == 0) & (h == 0)

    def yh_out(k):
        return kv_copy(place(OWN, k), place(YH, k), 1, k, yh_peer)

    def sib_out(k):
        return kv_copy(place(OWN, k), place(SIB, k), 2, k, sib_peer)

    def diag_out(k):
        return kv_copy(place(YH, k), place(DIAG, k), 3, k, sib_peer)

    def arrived(slot):
        kv_copy(slot, slot, 0, 0, sib_peer).wait_recv()

    def send(sends):
        for ok, copy in sends:
            pl.when(ok)(copy.start)

    def step_own(k):
        if k:
            pl.when(owned(k))(lambda: arrived(place(OWN, k)))
        if k == 2:
            send(third_sends())
        if k not in ACROSS:
            pl.when(owned(k) & yh_ok(k, 1 - h))(lambda: yh_out(k).start())
        pl.when(owned(k) & sib_ok(k, 1 - c))(lambda: sib_out(k).start())

    def step_yh(k):
        pl.when(yh_ok(k, h))(lambda: arrived(place(YH, k)))
        pl.when(diag_ok(k, 1 - c))(lambda: diag_out(k).start())

    def step_sib(*ks):
        for k in ks:
            pl.when(sib_ok(k, c))(lambda: arrived(place(SIB, k)))

    def step_diag(*ks):
        for k in ks:
            pl.when(diag_ok(k, c))(lambda: arrived(place(DIAG, k)))

    lane = lax.broadcasted_iota(jnp.int32, (TOK, TOK), 1)
    sub = lax.broadcasted_iota(jnp.int32, (TOK, TOK), 0)
    eye = lane == sub

    def part(j, a, first, count):
        q = qbuf[j, pl.ds(a * TOK, TOK), :]
        k = kv[rows_of(first, count), 0:HD]
        v = kv[rows_of(first, count), HD:]
        v = jnp.concatenate([v, jnp.ones_like(v)], axis=1)
        s = lax.dot_general(q, k, (((1,), (1,)), ((), ())), preferred_element_type=jnp.float32)
        p = jnp.exp2(jnp.tanh(s * FACTOR) * GAIN)
        start = starts[j]
        tiles = []
        for t in range(count):
            g, at = SLOT[first + t]
            k_of = 9 * (1 - c) if at == 0 and g in (SIB, DIAG) else ORDER[at]
            w_of = w + (1 - 2 * h if g in (YH, DIAG) else 0) + (2 - 4 * c if g in (SIB, DIAG) else 0)
            key_pos = (4 * (4 * (L - k_of) + w_of) + x) * TOK + lane
            ok = key_pos >= start
            if at == 0:
                ok = ok & (key_pos <= (4 * u + (x + j) % 4) * TOK + sub)
            tiles.append(jnp.where(ok, p[:, t * TOK:(t + 1) * TOK], 0.0).astype(jnp.bfloat16))
        return jnp.dot(jnp.concatenate(tiles, axis=1), v, preferred_element_type=jnp.float32)

    def add(j, first, count, fresh=False, heads=(0, HEADS)):
        def one(a, carry):
            rows = pl.ds(a * TOK, TOK)
            new = part(j, a, first, count)
            acc[j, rows, :] = new if fresh else acc[j, rows, :] + new
            return carry
        lax.fori_loop(*heads, one, 0, unroll=True)

    def give(j, half, first=None, count=0, passing=False):
        def one(a, carry):
            rows = pl.ds(a * TOK, TOK)
            total = acc[j, rows, :]
            if count:
                total = total + part(j, a, first, count)
            numerator = total[:, 0:HD]
            if passing:
                numerator = numerator + orecv[1, rows, :].astype(jnp.float32)
            osend[j - 1, rows, :] = numerator.astype(jnp.bfloat16)
            dsend[j - 1, pl.ds(a, 1), :] = jnp.sum(jnp.where(eye, total[:, HD:], 0.0), axis=0, keepdims=True)
            return carry
        lax.fori_loop(half * HEADS // 2, (half + 1) * HEADS // 2, one, 0, unroll=True)
        o_copy(j, half).start()

    def others(first, count, hooks, fresh=False):
        def one(i, carry):
            j = 1 + 2 * i
            if fresh:
                q_copy(j).wait_recv()
            add(j, first, count, fresh)
            for at, hook in enumerate(hooks):
                pl.when(i == at)(hook)
            return carry
        lax.fori_loop(0, 2, one, 0)

    def steps(*pairs):
        def run():
            for step, k in pairs:
                step(k)
        return run

    send(first_sends())
    step_own(0)
    q_copy(1).start()
    q_copy(3).start()

    for j in range(4):
        pos = (4 * u + (x + j) % 4) * TOK + lax.broadcasted_iota(jnp.int32, (TOK, TOK), 0)
        end = jnp.int32(0)
        start = jnp.zeros((TOK, TOK), jnp.int32)
        for d in range(NDOCS):
            length = lens[d]
            end = end + length
            start = start + jnp.where(pos >= end, length, 0)
        starts[j] = start

    step_own(1)
    step_own(8)
    step_sib(0, 1, 8)
    step_own(9)
    step_sib(9)
    add(0, 0, 6, fresh=True)
    q_copy(2).start()
    step_yh(0)
    step_yh(1)
    step_yh(8)
    step_own(2)
    step_own(7)
    send(second_sends())
    step_sib(2, 7)
    add(0, 6, 4)
    others(0, 10, [
        steps((step_yh, 9), (step_yh, 2), (step_yh, 7)),
        steps((step_own, 3), (step_own, 6)),
    ], fresh=True)
    step_diag(0, 1, 8, 9, 2, 7)
    others(10, 10, [
        steps((step_own, 5), (step_own, 4)),
        steps((step_yh, 3), (step_yh, 6)),
    ])
    q_copy(2).wait_recv()
    add(2, 0, 20, fresh=True)
    steps((step_yh, 5), (step_yh, 4))()
    step_sib(3, 6)
    step_diag(3, 6)
    add(0, 10, 10)
    step_sib(4, 5)
    step_diag(4, 5)
    give(2, 0, 20, 16)
    give(2, 1, 20, 16)
    d_copy(2).start()
    give(1, 1, 20, 16)
    give(3, 0, 20, 16)
    add(1, 20, 16, heads=(0, HEADS // 2))
    add(3, 20, 16, heads=(HEADS // 2, HEADS))
    o_copy(2, 0).wait_recv()
    give(1, 0, passing=True)
    o_copy(2, 1).wait_recv()
    give(3, 1, passing=True)
    d_copy(1).start()
    d_copy(3).start()
    add(0, 20, 16)

    for j in (2, 3, 1):
        d_copy(j).wait_recv()
    for a in range(HEADS):
        if a % (HEADS // 2) == 0:
            for j in (1, 3):
                o_copy(j, a // (HEADS // 2)).wait_recv()
        rows = slice(a * TOK, (a + 1) * TOK)
        num = acc[0, rows, 0:HD]
        den = drecv[0, a:a + 1, :] + drecv[1, a:a + 1, :] + drecv[2, a:a + 1, :]
        den = jnp.sum(jnp.where(eye, den, 0.0), axis=1, keepdims=True) + acc[0, rows, HD:]
        for j in (0, 2):
            num = num + orecv[j, rows, :].astype(jnp.float32)
        o_ref[:, a * HD:(a + 1) * HD] = (num / den).astype(jnp.bfloat16)

    for j in (1, 2, 3):
        q_copy(j).wait_send()
        o_copy(j, 0).wait_send()
        o_copy(j, 1).wait_send()
        d_copy(j).wait_send()
    for ok, copy in first_sends() + second_sends() + third_sends():
        pl.when(ok)(copy.wait_send)
    for k in range(10):
        if k not in ACROSS:
            pl.when(owned(k) & yh_ok(k, 1 - h))(lambda: yh_out(k).wait_send())
        pl.when(owned(k) & sib_ok(k, 1 - c))(lambda: sib_out(k).wait_send())
        pl.when(diag_ok(k, 1 - c))(lambda: diag_out(k).wait_send())


def per_device(queries, keys, values, doc_lengths):
    return pl.pallas_call(
        kernel,
        out_shape=jax.ShapeDtypeStruct((TOK, HEADS * HD), jnp.bfloat16),
        in_specs=[pl.BlockSpec(memory_space=pl.ANY)] * 4,
        out_specs=pl.BlockSpec(memory_space=pltpu.VMEM),
        scratch_shapes=[
            pltpu.SMEM((NDOCS,), jnp.int32),
            pltpu.SemaphoreType.DMA((3 + HEADS,)),
            pltpu.VMEM((len(SLOT) * TOK, 2 * HD), jnp.bfloat16),
            pltpu.VMEM((4, ROWS, HD), jnp.bfloat16),
            pltpu.VMEM((4, TOK, TOK), jnp.int32),
            pltpu.VMEM((4, ROWS, 2 * HD), jnp.float32),
            pltpu.VMEM((3, ROWS, HD), jnp.bfloat16),
            pltpu.VMEM((3, ROWS, HD), jnp.bfloat16),
            pltpu.VMEM((3, HEADS, TOK), jnp.float32),
            pltpu.VMEM((3, HEADS, TOK), jnp.float32),
            pltpu.SemaphoreType.DMA((len(SLOT),)),
            pltpu.SemaphoreType.DMA((4, 10)),
            pltpu.SemaphoreType.DMA((3,)),
            pltpu.SemaphoreType.DMA((3,)),
            pltpu.SemaphoreType.DMA((3, 2)),
            pltpu.SemaphoreType.DMA((3, 2)),
            pltpu.SemaphoreType.DMA((3,)),
            pltpu.SemaphoreType.DMA((3,)),
        ],
        compiler_params=pltpu.CompilerParams(
            collective_id=0, has_side_effects=True, vmem_limit_bytes=40 * 1024 * 1024),
        name="packed_attention",
    )(queries, keys, values, doc_lengths)


def solution(mesh):
    return jax.shard_map(
        per_device,
        mesh=mesh,
        in_specs=(
            P(("ctx", "head"), None),
            P(("ctx", "head"), None),
            P(("ctx", "head"), None),
            P(),
        ),
        out_specs=P(("ctx", "head"), None),
        check_vma=False,
    )
```

```python
import functools
import math

import jax
import jax.numpy as jnp
from jax import lax
from jax.experimental import pallas as pl
from jax.experimental.pallas import tpu as pltpu
from jax.sharding import PartitionSpec as P

MESH = pl.DeviceIdType.MESH
HD = 128
HEADS = 8
TOK = 128
NDOCS = 16
ROWS = HEADS * TOK
FACTOR = 1.0 / (30.0 * math.sqrt(HD))
GAIN = 30.0 * math.log2(math.e)
OWN, SIB, YH, DIAG = range(4)
ACROSS = (1, 8)
ORDER = (0, 1, 8, 2, 7, 3, 6, 4, 5)
EARLY = [(g, p) for g in (OWN, SIB) for p in (0, 1, 2)] + [(g, p) for g in (OWN, SIB) for p in (3, 4)]
EARLY += [(g, p) for g in (YH, DIAG) for p in (0, 1, 2)] + [(g, p) for g in (YH, DIAG) for p in (3, 4)]
LATE = [(g, p) for g in (OWN, SIB, YH, DIAG) for p in (5, 6)]
LATE += [(g, p) for g in (OWN, SIB, YH, DIAG) for p in (7, 8)]
SLOT = EARLY + LATE + [(OWN, 9), (YH, 9)]


def place(g, k):
    if k == 9:
        return SLOT.index((g, 9 if g in (OWN, YH) else 0))
    return SLOT.index((g, ORDER.index(k)))


def rows_of(slot, count=1):
    return pl.ds(slot * TOK, count * TOK)


def kernel(
    q_ref, k_ref, v_ref, len_ref, o_ref,
    lens, local, kv, qbuf, starts, acc, osend, orecv, dsend, drecv,
    kv_recv, kv_send, q_recv, q_send, o_recv, o_send, d_recv, d_send,
):
    ctx = lax.axis_index("ctx")
    head = lax.axis_index("head")
    L = ctx // 2
    z = L % 8
    c = ctx % 2
    h = head // 4
    x = head % 4
    w = 2 * c + h
    u = 4 * L + w

    other = (1 - h) * 4 + x
    yh_peer = (ctx, other)
    sib_peer = (L * 2 + 1 - c, head)

    def x_peer(j):
        return (ctx, h * 4 + (x + j) % 4)

    barrier = pltpu.get_barrier_semaphore()
    for peer in (yh_peer, sib_peer, x_peer(1), x_peer(2), x_peer(3)):
        pl.semaphore_signal(barrier, inc=1, device_id=peer, device_id_type=MESH)

    count = jnp.int32(5)
    for away in range(1, 10):
        from_ok, to_ok = L >= away, L + away < 16
        if away == 9:
            from_ok, to_ok = from_ok & (c == 1), to_ok & (c == 1)
        peers = [head] * (away not in (3, 4)) + [other] * (away in ACROSS)
        count = count + len(peers) * to_ok.astype(jnp.int32)

        @pl.when(from_ok)
        def _():
            for peer in peers:
                pl.semaphore_signal(
                    barrier, inc=1, device_id=(ctx - 2 * away, peer), device_id_type=MESH)

    loads = [
        pltpu.make_async_copy(k_ref, kv.at[rows_of(0), pl.ds(0, HD)], local.at[0]),
        pltpu.make_async_copy(v_ref, kv.at[rows_of(0), pl.ds(HD, HD)], local.at[1]),
        pltpu.make_async_copy(len_ref, lens, local.at[2]),
    ] + [
        pltpu.make_async_copy(
            q_ref.at[:, pl.ds(a * HD, HD)], qbuf.at[0, pl.ds(a * TOK, TOK)], local.at[3 + a])
        for a in range(HEADS)
    ]
    for load in loads:
        load.start()

    for slot, (g, p) in enumerate(EARLY + LATE):
        empty = L < ORDER[p]
        if p == 0 and g == SIB:
            empty = (c == 0) & (L < 9)
        if p == 0 and g == DIAG:
            empty = (c == 0) & ((L < 9) | (h == 1))
        if p == 0 and g in (OWN, YH):
            continue

        @pl.when(empty)
        def _():
            kv[rows_of(slot), :] = jnp.zeros((TOK, 2 * HD), kv.dtype)

    for load in loads:
        load.wait()

    pl.semaphore_wait(barrier, count)

    def q_copy(j):
        return pltpu.make_async_remote_copy(
            src_ref=qbuf.at[0], dst_ref=qbuf.at[j], send_sem=q_send.at[j - 1],
            recv_sem=q_recv.at[j - 1], device_id=x_peer(4 - j), device_id_type=MESH)

    def o_copy(j, half):
        rows = pl.ds(half * (ROWS // 2), ROWS // 2)
        return pltpu.make_async_remote_copy(
            src_ref=osend.at[j - 1, rows], dst_ref=orecv.at[j - 1, rows], send_sem=o_send.at[j - 1, half],
            recv_sem=o_recv.at[j - 1, half], device_id=x_peer(j if j != 2 else 1 + 2 * half),
            device_id_type=MESH)

    def d_copy(j):
        return pltpu.make_async_remote_copy(
            src_ref=dsend.at[j - 1], dst_ref=drecv.at[j - 1], send_sem=d_send.at[j - 1],
            recv_sem=d_recv.at[j - 1], device_id=x_peer(j), device_id_type=MESH)

    def kv_copy(src, dst, kind, k, peer):
        return pltpu.make_async_remote_copy(
            src_ref=kv.at[rows_of(src)], dst_ref=kv.at[rows_of(dst)], send_sem=kv_send.at[kind, k],
            recv_sem=kv_recv.at[dst], device_id=peer, device_id_type=MESH)

    def owned(k):
        return L >= k if k <= 8 else (L >= k) & (c == 1)

    def out(k, to_k, across=False):
        return kv_copy(
            place(OWN, k), place(YH if across else OWN, to_k), 1 if across else 0, to_k,
            (ctx + 2 * (to_k - k), other if across else head))

    def first_sends():
        sends = [(L + 1 < 16, out(0, 1)), (L + 8 < 16, out(0, 8))]
        sends += [(L + 1 < 16, out(0, 1, True)), (L + 8 < 16, out(0, 8, True))]
        sends += [(L + 2 < 16, out(0, 2)), (L + 7 < 16, out(0, 7)), ((L + 9 < 16) & (c == 1), out(0, 9))]
        return sends

    def second_sends():
        return [(L + 6 < 16, out(0, 6)), (L + 5 < 16, out(0, 5))]

    def third_sends():
        return [((L >= 2) & (L + 1 < 16), out(2, 3)), ((L >= 2) & (L + 2 < 16), out(2, 4))]

    def yh_ok(k, to_h):
        return L >= k if k <= 8 else (L >= k) & (c == 1) & (to_h == 0)

    def sib_ok(k, to_c):
        if k in (0, 9):
            return (L >= k) & (to_c == (0 if k else 1))
        return L >= k

    def diag_ok(k, to_c):
        if k == 0:
            return to_c == 1
        return L >= k if k <= 8 else (L >= k) & (to_c == 0) & (h == 0)

    def yh_out(k):
        return kv_copy(place(OWN, k), place(YH, k), 1, k, yh_peer)

    def sib_out(k):
        return kv_copy(place(OWN, k), place(SIB, k), 2, k, sib_peer)

    def diag_out(k):
        return kv_copy(place(YH, k), place(DIAG, k), 3, k, sib_peer)

    def arrived(slot):
        kv_copy(slot, slot, 0, 0, sib_peer).wait_recv()

    def send(sends):
        for ok, copy in sends:
            pl.when(ok)(copy.start)

    def step_own(k):
        if k:
            pl.when(owned(k))(lambda: arrived(place(OWN, k)))
        if k == 2:
            send(third_sends())
        if k not in ACROSS:
            pl.when(owned(k) & yh_ok(k, 1 - h))(lambda: yh_out(k).start())
        pl.when(owned(k) & sib_ok(k, 1 - c))(lambda: sib_out(k).start())

    def step_yh(k):
        pl.when(yh_ok(k, h))(lambda: arrived(place(YH, k)))
        pl.when(diag_ok(k, 1 - c))(lambda: diag_out(k).start())

    def step_sib(*ks):
        for k in ks:
            pl.when(sib_ok(k, c))(lambda: arrived(place(SIB, k)))

    def step_diag(*ks):
        for k in ks:
            pl.when(diag_ok(k, c))(lambda: arrived(place(DIAG, k)))

    lane = lax.broadcasted_iota(jnp.int32, (TOK, TOK), 1)
    sub = lax.broadcasted_iota(jnp.int32, (TOK, TOK), 0)
    eye = lane == sub

    def part(j, a, first, count):
        q = qbuf[j, pl.ds(a * TOK, TOK), :]
        k = kv[rows_of(first, count), 0:HD]
        v = kv[rows_of(first, count), HD:]
        v = jnp.concatenate([v, jnp.ones_like(v)], axis=1)
        s = lax.dot_general(q, k, (((1,), (1,)), ((), ())), preferred_element_type=jnp.float32)
        p = jnp.exp2(jnp.tanh(s * FACTOR) * GAIN)
        start = starts[j]
        tiles = []
        for t in range(count):
            g, at = SLOT[first + t]
            k_of = 9 * (1 - c) if at == 0 and g in (SIB, DIAG) else ORDER[at]
            w_of = w + (1 - 2 * h if g in (YH, DIAG) else 0) + (2 - 4 * c if g in (SIB, DIAG) else 0)
            key_pos = (4 * (4 * (L - k_of) + w_of) + x) * TOK
            ok = start <= key_pos
            if at == 0:
                ok = ok & (lane - sub <= (4 * u + (x + j) % 4) * TOK - key_pos)
            tiles.append(jnp.where(ok, p[:, t * TOK:(t + 1) * TOK], 0.0).astype(jnp.bfloat16))
        return jnp.dot(jnp.concatenate(tiles, axis=1), v, preferred_element_type=jnp.float32)

    def add(j, first, count, fresh=False, heads=(0, HEADS)):
        def one(a, carry):
            rows = pl.ds(a * TOK, TOK)
            new = part(j, a, first, count)
            acc[j, rows, :] = new if fresh else acc[j, rows, :] + new
            return carry
        lax.fori_loop(*heads, one, 0, unroll=True)

    def give(j, half, first=None, count=0, passing=False):
        def one(a, carry):
            rows = pl.ds(a * TOK, TOK)
            total = acc[j, rows, :]
            if count:
                total = total + part(j, a, first, count)
            numerator = total[:, 0:HD]
            if passing:
                numerator = numerator + orecv[1, rows, :].astype(jnp.float32)
            osend[j - 1, rows, :] = numerator.astype(jnp.bfloat16)
            dsend[j - 1, pl.ds(a, 1), :] = jnp.sum(jnp.where(eye, total[:, HD:], 0.0), axis=0, keepdims=True)
            return carry
        lax.fori_loop(half * HEADS // 2, (half + 1) * HEADS // 2, one, 0, unroll=True)
        o_copy(j, half).start()

    def others(first, count, hooks, fresh=False):
        def one(i, carry):
            j = 1 + (2 * i) % 3
            if fresh:
                q_copy(j).wait_recv()
            add(j, first, count, fresh)
            for at, hook in enumerate(hooks):
                pl.when(i == at)(hook)
            return carry
        lax.fori_loop(0, 3, one, 0)

    def steps(*pairs):
        def run():
            for step, k in pairs:
                step(k)
        return run

    send(first_sends())
    step_own(0)
    q_copy(1).start()
    q_copy(3).start()

    for j in range(4):
        pos = (4 * u + (x + j) % 4) * TOK + lax.broadcasted_iota(jnp.int32, (TOK, TOK), 0)
        end = jnp.int32(0)
        start = jnp.zeros((TOK, TOK), jnp.int32)
        for d in range(NDOCS):
            length = lens[d]
            end = end + length
            start = start + jnp.where(pos >= end, length, 0)
        starts[j] = start - lane

    step_own(1)
    step_own(8)
    step_sib(0, 1, 8)
    step_own(9)
    step_sib(9)
    add(0, 0, 6, fresh=True)
    q_copy(2).start()
    step_yh(0)
    step_yh(1)
    step_yh(8)
    step_own(2)
    step_own(7)
    send(second_sends())
    step_sib(2, 7)
    add(0, 6, 4)
    others(0, 10, [
        steps((step_yh, 9), (step_yh, 2), (step_yh, 7)),
        steps((step_own, 3), (step_own, 6)),
        steps((step_diag, 0), (step_diag, 1), (step_diag, 8), (step_diag, 9), (step_diag, 2), (step_diag, 7)),
    ], fresh=True)
    others(10, 10, [
        steps((step_own, 5), (step_own, 4)),
        steps((step_yh, 3), (step_yh, 6)),
        steps((step_sib, 3), (step_sib, 6), (step_diag, 3), (step_diag, 6)),
    ])
    others(20, 8, [
        steps((step_yh, 5), (step_yh, 4)),
        steps(),
        steps((step_sib, 4), (step_sib, 5), (step_diag, 4), (step_diag, 5)),
    ])

    give(2, 0, 28, 8)
    give(2, 1, 28, 8)
    d_copy(2).start()
    give(1, 1, 28, 8)
    give(3, 0, 28, 8)
    add(1, 28, 8, heads=(0, HEADS // 2))
    add(3, 28, 8, heads=(HEADS // 2, HEADS))
    add(0, 10, 10)
    o_copy(2, 0).wait_recv()
    give(1, 0, passing=True)
    o_copy(2, 1).wait_recv()
    give(3, 1, passing=True)
    d_copy(1).start()
    d_copy(3).start()
    add(0, 20, 16)

    for j in (2, 3, 1):
        d_copy(j).wait_recv()
    for a in range(HEADS):
        if a % (HEADS // 2) == 0:
            for j in (1, 3):
                o_copy(j, a // (HEADS // 2)).wait_recv()
        rows = slice(a * TOK, (a + 1) * TOK)
        num = acc[0, rows, 0:HD]
        den = drecv[0, a:a + 1, :] + drecv[1, a:a + 1, :] + drecv[2, a:a + 1, :]
        den = jnp.sum(jnp.where(eye, den, 0.0), axis=1, keepdims=True) + acc[0, rows, HD:]
        for j in (0, 2):
            num = num + orecv[j, rows, :].astype(jnp.float32)
        o_ref[:, a * HD:(a + 1) * HD] = (num / den).astype(jnp.bfloat16)

    for j in (1, 2, 3):
        q_copy(j).wait_send()
        o_copy(j, 0).wait_send()
        o_copy(j, 1).wait_send()
        d_copy(j).wait_send()
    for ok, copy in first_sends() + second_sends() + third_sends():
        pl.when(ok)(copy.wait_send)
    for k in range(10):
        if k not in ACROSS:
            pl.when(owned(k) & yh_ok(k, 1 - h))(lambda: yh_out(k).wait_send())
        pl.when(owned(k) & sib_ok(k, 1 - c))(lambda: sib_out(k).wait_send())
        pl.when(diag_ok(k, 1 - c))(lambda: diag_out(k).wait_send())


def per_device(queries, keys, values, doc_lengths):
    return pl.pallas_call(
        kernel,
        out_shape=jax.ShapeDtypeStruct((TOK, HEADS * HD), jnp.bfloat16),
        in_specs=[pl.BlockSpec(memory_space=pl.ANY)] * 4,
        out_specs=pl.BlockSpec(memory_space=pltpu.VMEM),
        scratch_shapes=[
            pltpu.SMEM((NDOCS,), jnp.int32),
            pltpu.SemaphoreType.DMA((3 + HEADS,)),
            pltpu.VMEM((len(SLOT) * TOK, 2 * HD), jnp.bfloat16),
            pltpu.VMEM((4, ROWS, HD), jnp.bfloat16),
            pltpu.VMEM((4, TOK, TOK), jnp.int32),
            pltpu.VMEM((4, ROWS, 2 * HD), jnp.float32),
            pltpu.VMEM((3, ROWS, HD), jnp.bfloat16),
            pltpu.VMEM((3, ROWS, HD), jnp.bfloat16),
            pltpu.VMEM((3, HEADS, TOK), jnp.float32),
            pltpu.VMEM((3, HEADS, TOK), jnp.float32),
            pltpu.SemaphoreType.DMA((len(SLOT),)),
            pltpu.SemaphoreType.DMA((4, 10)),
            pltpu.SemaphoreType.DMA((3,)),
            pltpu.SemaphoreType.DMA((3,)),
            pltpu.SemaphoreType.DMA((3, 2)),
            pltpu.SemaphoreType.DMA((3, 2)),
            pltpu.SemaphoreType.DMA((3,)),
            pltpu.SemaphoreType.DMA((3,)),
        ],
        compiler_params=pltpu.CompilerParams(
            collective_id=0, has_side_effects=True, vmem_limit_bytes=40 * 1024 * 1024),
        name="packed_attention",
    )(queries, keys, values, doc_lengths)


def solution(mesh):
    return jax.shard_map(
        per_device,
        mesh=mesh,
        in_specs=(
            P(("ctx", "head"), None),
            P(("ctx", "head"), None),
            P(("ctx", "head"), None),
            P(),
        ),
        out_specs=P(("ctx", "head"), None),
        check_vma=False,
    )
```
